256 devices in a mesh: gx: 16 (over x_lo, y, core), gy: 8 (over z), gz: 2 (over x_hi).
Axes of the slice: x: 4 (x_hi: 2, x_lo: 2; x = x_hi * 2 + x_lo), y: 4, z: 8, core: 2. Of those that a mesh axis runs over, the one named last changes fastest.
Arguments:
- fields: float32 [5, 2, 4096, 4096], P(None, 'gz', 'gx', 'gy'), parts along dimension 1, may hold values from -6 to 6
Outputs:
- deriv_x: float32 [5, 2, 4096, 4096], P(None, 'gz', 'gx', 'gy'), parts along dimension 1
- deriv_y: float32 [5, 2, 4096, 4096], P(None, 'gz', ('gx', 'gy')), parts along dimension 1
The draws below stay inside these ranges and needn't reach their ends.
There are 2 independent parts, one for each index of `gz`. The reference program is written for one: setup_inputs(seed, part) draws one part's arguments, and reference() takes and returns one part's arrays. A program takes and returns all parts, laid end to end along the dimension named above; each array names one. Nothing has to cross between parts.
All inputs are finite; a program needn't handle non-finite values.
Results may differ from the reference program's by a relative error of at most 0.00002.
Values sent between devices are 32-bit elements; how exact they have to be, the bound alone decides.
No kernel may reach another device: no remote copies, remote signals or barrier semaphores. Data moves between devices by JAX's collectives and lax.ppermute only.
A program may use at most 64 MiB of HBM per device.

```python
import jax
import jax.numpy as jnp

FIELDS = 5
NX = 4096
NY = 4096
ZS = 1
LEVELS = 4


def block_levels(rng, dims, split, low, high):
    factor_of = 1.0
    for axis_at, parts in split:
        steps = jax.random.uniform(jax.random.fold_in(jax.random.fold_in(rng, 6), axis_at), (parts,), jnp.float32, low / len(split), high / len(split))
        factor_of = factor_of * jnp.repeat(jnp.exp(steps), dims[axis_at] // parts).reshape((-1,) + (1,) * (len(dims) - 1 - axis_at))
    return factor_of


def normal_values(key, shape, spread, bound, shards=(), dtype=jnp.bfloat16):
    result = jax.random.normal(key, shape, jnp.float32) * spread
    if len(shards) > 0:
        result = block_levels(key, shape, shards, -0.22, 0.18) * result
    return jnp.clip(result, min=-bound, max=bound).astype(dtype)


def setup_inputs(seed: int = 0, part: int = 0) -> dict:
    key_list = jax.random.split(jax.random.key(seed), 2)
    part_splits = jax.random.split(jax.random.fold_in(key_list[1], part), 2)
    return {
        "fields": normal_values(part_splits[0], (FIELDS, ZS, NX, NY), 1.0, 6.0, ((2, 16), (3, 8)), jnp.float32),
    }


def coefficients(levels):
    upper = 1.0 / 3.0
    middle = 1.0
    factors = []
    for level in range(levels):
        factor = upper / middle
        factors.append(factor)
        middle = middle - 2.0 * factor * upper
        upper = -factor * upper
    return factors, middle


def right_side(field, axis):
    ahead = jnp.roll(field, -1, axis) - jnp.roll(field, 1, axis)
    farther = jnp.roll(field, -2, axis) - jnp.roll(field, 2, axis)
    return (7.0 / 9.0) * ahead + (1.0 / 36.0) * farther


def reduce_solve(values, axis):
    factors, middle = coefficients(LEVELS)
    for level in range(LEVELS):
        stride = 2 ** level
        values = values - factors[level] * (jnp.roll(values, stride, axis) + jnp.roll(values, -stride, axis))
    return values / middle


def reference(fields):
    deriv_x = reduce_solve(right_side(fields, 2), 2)
    deriv_y = reduce_solve(right_side(fields, 3), 3)
    return deriv_x, deriv_y
```

```python
import jax
import jax.numpy as jnp
from jax import lax
from jax.experimental import pallas as pl
from jax.experimental.pallas import tpu as pltpu
from jax.sharding import PartitionSpec as P

LEVELS = 4
HALO = 24
LANES = 128
SUBLANES = 8
ORDER = (4, 3, 5, 2, 6, 1, 7)


def coefficients(levels):
    upper = 1.0 / 3.0
    middle = 1.0
    factors = []
    for level in range(levels):
        factor = upper / middle
        factors.append(factor)
        middle = middle - 2.0 * factor * upper
        upper = -factor * upper
    return (factors, middle)


def derivative(cells, axis):
    length = cells.shape[axis]

    def shifted(values, offset):
        return pltpu.roll(values, (-offset) % length, axis)

    factors, middle = coefficients(LEVELS)
    values = 7.0 / 9.0 * (shifted(cells, 1) - shifted(cells, -1)) + 1.0 / 36.0 * (
        shifted(cells, 2) - shifted(cells, -2)
    )
    for level in range(LEVELS):
        stride = 2**level
        values = values - factors[level] * (shifted(values, stride) + shifted(values, -stride))
    return values * (1.0 / middle)


def x_kernel(cells, below, above, out):
    fields, _, rows, columns = cells.shape
    tiles = columns // LANES

    def step(index, carry):
        field = index // tiles
        at = pl.ds(pl.multiple_of((index % tiles) * LANES, LANES), LANES)
        extended = jnp.concatenate(
            [below[field, 0, :, at], cells[field, 0, :, at], above[field, 0, :, at]], axis=0
        )
        out[field, 0, :, at] = derivative(extended, 0)[HALO : HALO + rows]
        return carry

    lax.fori_loop(0, fields * tiles, step, 0)


def y_kernel(*refs):
    parts = refs[:-3]
    out, result, sems = refs[-3:]
    count = len(parts)
    me = lax.axis_index("gy")
    fields, _, rows, columns = parts[0].shape
    groups = rows // SUBLANES

    def step(index, carry):
        field = index // groups
        at = pl.ds(pl.multiple_of((index % groups) * SUBLANES, SUBLANES), SUBLANES)
        row = jnp.concatenate([part[field, 0, at, :] for part in parts], axis=1)
        solved = derivative(row, 1)
        for part in range(count):
            column = pl.multiple_of(lax.rem(me + part, count) * columns, columns)
            result[field, 0, at, pl.ds(column, columns)] = solved[:, part * columns : (part + 1) * columns]
        return carry

    copies = []
    for field in range(fields):
        lax.fori_loop(field * groups, (field + 1) * groups, step, 0)
        copy = pltpu.make_async_copy(result.at[field], out.at[field], sems.at[field])
        copy.start()
        copies.append(copy)
    for copy in copies:
        copy.wait()


def body(fields):
    count = lax.axis_size("gy")
    ring = lax.axis_size("gx")
    me = lax.axis_index("gy")
    depth, slab, rows, columns = fields.shape
    part = rows // count

    def block(owner):
        return lax.dynamic_slice_in_dim(fields, lax.rem(owner, count) * part, part, 2)

    parts = [block(me)] + [None] * (count - 1)
    for hop in ORDER:
        parts[count - hop] = lax.ppermute(
            block(me + hop), "gy", [(i, (i + hop) % count) for i in range(count)]
        )
    below = lax.ppermute(fields[:, :, rows - HALO :], "gx", [(i, (i + 1) % ring) for i in range(ring)])
    above = lax.ppermute(fields[:, :, :HALO], "gx", [((i + 1) % ring, i) for i in range(ring)])
    vmem = pl.BlockSpec(memory_space=pltpu.VMEM)
    deriv_x = pl.pallas_call(
        x_kernel,
        out_shape=jax.ShapeDtypeStruct(fields.shape, fields.dtype),
        in_specs=[vmem] * 3,
        out_specs=vmem,
        cost_estimate=pl.CostEstimate(
            flops=20 * fields.size, bytes_accessed=8 * fields.size, transcendentals=0
        ),
    )(fields, below, above)
    deriv_y = pl.pallas_call(
        y_kernel,
        out_shape=jax.ShapeDtypeStruct((depth, slab, part, count * columns), fields.dtype),
        in_specs=[vmem] * count,
        out_specs=pl.BlockSpec(memory_space=pl.ANY),
        scratch_shapes=[
            pltpu.VMEM((depth, slab, part, count * columns), jnp.float32),
            pltpu.SemaphoreType.DMA((depth,)),
        ],
        cost_estimate=pl.CostEstimate(
            flops=20 * fields.size, bytes_accessed=8 * fields.size, transcendentals=0
        ),
    )(*parts)
    return (deriv_x, deriv_y)


def solution(mesh):
    placed = (P(None, "gz", "gx", "gy"),)
    return jax.shard_map(
        body,
        mesh=mesh,
        in_specs=placed,
        out_specs=(P(None, "gz", "gx", "gy"), P(None, "gz", ("gx", "gy"), None)),
        check_vma=False,
    )
```

```python
import jax
import jax.numpy as jnp
import numpy as np
from jax import lax
from jax.experimental import pallas as pl
from jax.experimental.pallas import tpu as pltpu
from jax.sharding import PartitionSpec as P

LEVELS = 4
HALO = 24
LIMIT = 16 * 2**20
STEPS = (
    ("y4", ()),
    ("b", ()),
    ("a", ()),
    ("X", ()),
    ("y3", ()),
    ("y5", ()),
    ("y2", ("y4", "b", )),
    ("y6", ("y4", "a", )),
    ("y1", ("y3", "X", )),
    ("y7", ("y5", )),
    ("A", ()),
    ("B", ()),
    ("C", ()),
)
GROUPS = ((4,), (3, 5), (2, 6, 1, 7, 0))
LANES = 128
UNIT = 256
REACH = 17


def coefficients(levels):
    upper = 1.0 / 3.0
    middle = 1.0
    factors = []
    for level in range(levels):
        factor = upper / middle
        factors.append(factor)
        middle = middle - 2.0 * factor * upper
        upper = -factor * upper
    return (factors, middle)


def band():
    taps = np.zeros(2 * REACH + 1)
    for offset, weight in ((1, 7.0 / 9.0), (2, 1.0 / 36.0)):
        taps[REACH + offset] = weight
        taps[REACH - offset] = -weight
    factors, middle = coefficients(LEVELS)
    for level in range(LEVELS):
        stride = 2**level
        last = taps
        taps = last.copy()
        taps[stride:] -= factors[level] * last[:-stride]
        taps[:-stride] -= factors[level] * last[stride:]
    matrix = np.zeros((UNIT + 2 * LANES, UNIT))
    for column in range(UNIT):
        first = LANES + column - REACH
        matrix[first : first + 2 * REACH + 1, column] = taps / middle
    return matrix.astype(np.float32)


def derivative(cells, axis):
    length = cells.shape[axis]

    def shifted(values, offset):
        return pltpu.roll(values, (-offset) % length, axis)

    factors, middle = coefficients(LEVELS)
    values = 7.0 / 9.0 * (shifted(cells, 1) - shifted(cells, -1)) + 1.0 / 36.0 * (
        shifted(cells, 2) - shifted(cells, -2)
    )
    for level in range(LEVELS):
        stride = 2**level
        values = values - factors[level] * (shifted(values, stride) + shifted(values, -stride))
    return values * (1.0 / middle)


def x_kernel(cells, below, above, out):
    fields, _, rows, columns = cells.shape
    tiles = columns // LANES

    def step(index, carry):
        field = index // tiles
        at = pl.ds(pl.multiple_of((index % tiles) * LANES, LANES), LANES)
        extended = jnp.concatenate(
            [below[field, 0, :, at], cells[field, 0, :, at], above[field, 0, :, at]], axis=0
        )
        out[field, 0, :, at] = derivative(extended, 0)[HALO : HALO + rows]
        return carry

    lax.fori_loop(0, fields * tiles, step, 0)


def cut_kernel(count, hops, chunks):
    def kernel(fields, *refs):
        outs, sems = refs[:-1], refs[-1]
        me = lax.axis_index("gy")
        copies = []
        for first, last in chunks:
            for hop in hops:
                rows = outs[len(copies)].shape[2]
                at = pl.multiple_of(lax.rem(me + hop, count) * rows, rows)
                copy = pltpu.make_async_copy(
                    fields.at[first:last, :, pl.ds(at, rows), :], outs[len(copies)], sems.at[len(copies)]
                )
                copy.start()
                copies.append(copy)
        for copy in copies:
            copy.wait()

    return kernel


def terms(values):
    high = values.astype(jnp.bfloat16)
    rest = values - high.astype(jnp.float32)
    middle = rest.astype(jnp.bfloat16)
    low = (rest - middle.astype(jnp.float32)).astype(jnp.bfloat16)
    return (high, middle, low)


def product(one, other, pairs):
    total = None
    for i, j in pairs:
        term = jnp.dot(one[i], other[j], preferred_element_type=jnp.float32)
        total = term if total is None else total + term
    return total


FULL = ((2, 0), (0, 2), (1, 1), (1, 0), (0, 1), (0, 0))
SHORT = ((1, 0), (0, 1), (0, 0))


def y_kernel(count, places, spans, aliased):
    def kernel(*refs):
        number = len(places)
        blocks = dict(zip(places, refs))
        inner = [ref[...] for ref in refs[number : number + 3]]
        outer = [ref[...] for ref in refs[number + 3 : number + 6]]
        out, result, sems = refs[number + 6 + aliased :]
        fields, _, rows, columns = refs[0].shape
        total = count * columns
        me = lax.axis_index("gy")
        copies = []

        def piece(lane):
            block, at = divmod(lane % total, columns)
            return terms(blocks[block][:, 0, :, at : at + LANES].reshape(fields * rows, LANES))

        def send(first, last, base):
            block, at = divmod(first % total, columns)
            to = pl.multiple_of(lax.rem(me + block, count) * columns + at, LANES)
            copy = pltpu.make_async_copy(
                result.at[:, :, :, pl.ds(base, last - first)],
                out.at[:, :, :, pl.ds(to, last - first)],
                sems.at[len(copies)],
            )
            copy.start()
            copies.append(copy)

        base = 0
        for first, last in spans:
            sent = first
            tile = {lane: piece(lane) for lane in range(first - LANES, first + LANES, LANES)}
            for lane in range(first, last, UNIT):
                for step in (lane + LANES, lane + UNIT):
                    if step not in tile:
                        tile[step] = piece(step)
                middle = [jnp.concatenate([tile[lane][t], tile[lane + LANES][t]], axis=1) for t in range(3)]
                sides = [jnp.concatenate([tile[lane - LANES][t], tile[lane + UNIT][t]], axis=1) for t in range(2)]
                solved = product(sides, outer, SHORT) + product(middle, inner, FULL)
                at = base + lane - first
                result[:, 0, :, at : at + UNIT] = solved.reshape(fields, rows, UNIT)
                edge = min((sent // columns + 1) * columns, last)
                while edge <= lane + UNIT and sent < edge:
                    send(sent, edge, base + sent - first)
                    sent, edge = edge, min((edge // columns + 1) * columns, last)
            base += last - first
        for copy in copies:
            copy.wait()

    return kernel


def y_call(parts, count, places, spans, matrices, partial):
    operands = [*(parts[place] for place in places), *matrices]
    fields, slab, rows, columns = operands[0].shape
    width = sum(last - first for first, last in spans)
    pieces = sum(-(-last // columns) - first // columns for first, last in spans)
    vmem = pl.BlockSpec(memory_space=pltpu.VMEM)
    hbm = pl.BlockSpec(memory_space=pl.ANY)
    aliased = partial is not None
    size = fields * rows * width
    return pl.pallas_call(
        y_kernel(count, places, spans, int(aliased)),
        out_shape=jax.ShapeDtypeStruct((fields, slab, rows, count * columns), jnp.float32),
        in_specs=[vmem] * len(operands) + [hbm] * aliased,
        out_specs=hbm,
        scratch_shapes=[
            pltpu.VMEM((fields, slab, rows, width), jnp.float32),
            pltpu.SemaphoreType.DMA((pieces,)),
        ],
        input_output_aliases={len(operands): 0} if aliased else {},
        compiler_params=pltpu.CompilerParams(vmem_limit_bytes=LIMIT),
        cost_estimate=pl.CostEstimate(
            flops=9 * 2 * 256 * size, bytes_accessed=8 * size, transcendentals=0
        ),
    )(*[pltpu.with_memory_space_constraint(x, pltpu.VMEM) for x in operands], *([partial] if aliased else []))


def split_band():
    matrix = band()
    inner = matrix[LANES : LANES + UNIT]
    outer = np.concatenate([matrix[:LANES], matrix[LANES + UNIT :]], axis=0)
    pieces = []
    for values in (inner, outer):
        for _ in range(3):
            piece = values.astype(jnp.bfloat16)
            values = values - piece.astype(np.float32)
            pieces.append(jnp.asarray(piece))
    return pieces


def body(fields):
    count = lax.axis_size("gy")
    ring = lax.axis_size("gx")
    depth, slab, rows, columns = fields.shape
    part = rows // count
    value = {}
    matrices = split_band()
    source = pltpu.with_memory_space_constraint(fields, pltpu.HBM)
    cuts = {}
    for group in GROUPS:
        number = len(group)
        got = pl.pallas_call(
            cut_kernel(count, group, ((0, depth),)),
            out_shape=[pltpu.VMEM((depth, slab, part, columns), jnp.float32)] * number,
            in_specs=[pl.BlockSpec(memory_space=pl.ANY)],
            out_specs=[pl.BlockSpec(memory_space=pltpu.VMEM)] * number,
            scratch_shapes=[pltpu.SemaphoreType.DMA((number,))],
            compiler_params=pltpu.CompilerParams(vmem_limit_bytes=2**23),
            cost_estimate=pl.CostEstimate(flops=0, bytes_accessed=2 * 4 * number * depth * part * columns, transcendentals=0),
        )(source)
        cuts.update(zip(group, got))
        if group is not GROUPS[-1]:
            fields, cuts[group[-1]] = lax.optimization_barrier((fields, cuts[group[-1]]))
            source = pltpu.with_memory_space_constraint(fields, pltpu.HBM)
    value["y0"] = cuts[0]
    vmem = pl.BlockSpec(memory_space=pltpu.VMEM)
    c, e = columns, LANES
    plans = {
        3: {
            "A": ([3, 4, 5, 0], ((3 * c + e, 6 * c - e), (8 * c + e, 9 * c - e))),
            "B": ([2, 3, 5, 6], ((2 * c + e, 3 * c + e), (6 * c - e, 7 * c - e))),
            "C": ([6, 7, 0, 1, 2], ((7 * c - e, 8 * c + e), (9 * c - e, 10 * c + e))),
        },
        2: {
            "A": ([2, 3, 4, 5, 6, 0], ((2 * c + e, 7 * c - e), (8 * c + e, 9 * c - e))),
            "C": ([6, 7, 0, 1, 2], ((7 * c - e, 8 * c + e), (9 * c - e, 10 * c + e))),
        },
        4: {
            "A": ([3, 2, 1, 0, 7, 6, 5], ((5 * c + e, 12 * c - e),)),
            "C": ([3, 4, 5], ((4 * c - e, 5 * c + e),)),
        },
    }[3]
    last = None

    def tie(x, deps):
        for dep in deps:
            x, value[dep] = lax.optimization_barrier((x, value[dep]))
        return x

    for name, deps in STEPS:
        if name[0] == "y":
            hop = int(name[1:])
            cut = tie(cuts[hop], deps)
            value[name] = lax.ppermute(cut, "gy", [(i, (i + hop) % count) for i in range(count)])
        elif name == "b":
            halo = tie(fields[:, :, rows - HALO :], deps)
            value[name] = lax.ppermute(halo, "gx", [(i, (i + 1) % ring) for i in range(ring)])
        elif name == "a":
            halo = tie(fields[:, :, :HALO], deps)
            value[name] = lax.ppermute(halo, "gx", [((i + 1) % ring, i) for i in range(ring)])
        elif name == "X":
            value[name] = pl.pallas_call(
                x_kernel,
                out_shape=jax.ShapeDtypeStruct(fields.shape, fields.dtype),
                in_specs=[vmem] * 3,
                out_specs=vmem,
                cost_estimate=pl.CostEstimate(
                    flops=20 * fields.size, bytes_accessed=8 * fields.size, transcendentals=0
                ),
            )(fields, tie(value["b"], deps), value["a"])
        else:
            places, spans = plans[name]
            parts = {place: value["y%d" % ((count - place) % count)] for place in places}
            parts[places[0]] = tie(parts[places[0]], deps)
            last = y_call(parts, count, places, spans, matrices, last)
            value[name] = last
    return (value["X"], last)


def solution(mesh):
    placed = (P(None, "gz", "gx", "gy"),)
    return jax.shard_map(
        body,
        mesh=mesh,
        in_specs=placed,
        out_specs=(P(None, "gz", "gx", "gy"), P(None, "gz", ("gx", "gy"), None)),
        check_vma=False,
    )
```

```python
import jax
import jax.numpy as jnp
import numpy as np
from jax import lax
from jax.experimental import pallas as pl
from jax.experimental.pallas import tpu as pltpu
from jax.sharding import PartitionSpec as P

LEVELS = 4
HALO = 24
LIMIT = 8 * 2**20
STACK = 400
STEPS = (
    ("y4", ()),
    ("b", ()),
    ("a", ()),
    ("X", ()),
    ("y3", ()),
    ("y5", ()),
    ("y2", ("y4", "b", )),
    ("y6", ("y4", "a", )),
    ("y1p", ("y3", "X", )),
    ("y7p", ("y5", )),
    ("y1q", ("y3", )),
    ("y7q", ("y6", )),
    ("A", ()),
    ("B", ()),
    ("C", ()),
    ("D", ()),
)
GROUPS = ((4,), (3, 5), (2, 6, "1p", "7p", "1q", "7q", 0))
SPLIT = 3
XLIMIT = 12 * 2**20
LANES = 128
UNIT = 256
REACH = 17


def coefficients(levels):
    upper = 1.0 / 3.0
    middle = 1.0
    factors = []
    for level in range(levels):
        factor = upper / middle
        factors.append(factor)
        middle = middle - 2.0 * factor * upper
        upper = -factor * upper
    return (factors, middle)


def band():
    taps = np.zeros(2 * REACH + 1)
    for offset, weight in ((1, 7.0 / 9.0), (2, 1.0 / 36.0)):
        taps[REACH + offset] = weight
        taps[REACH - offset] = -weight
    factors, middle = coefficients(LEVELS)
    for level in range(LEVELS):
        stride = 2**level
        last = taps
        taps = last.copy()
        taps[stride:] -= factors[level] * last[:-stride]
        taps[:-stride] -= factors[level] * last[stride:]
    matrix = np.zeros((UNIT + 2 * LANES, UNIT))
    for column in range(UNIT):
        first = LANES + column - REACH
        matrix[first : first + 2 * REACH + 1, column] = taps / middle
    return matrix.astype(np.float32)


def derivative(cells, axis):
    length = cells.shape[axis]

    def shifted(values, offset):
        return pltpu.roll(values, (-offset) % length, axis)

    factors, middle = coefficients(LEVELS)
    values = 7.0 / 9.0 * (shifted(cells, 1) - shifted(cells, -1)) + 1.0 / 36.0 * (
        shifted(cells, 2) - shifted(cells, -2)
    )
    for level in range(LEVELS):
        stride = 2**level
        values = values - factors[level] * (shifted(values, stride) + shifted(values, -stride))
    return values * (1.0 / middle)


def x_kernel(cells, below, above, out):
    fields, _, rows, columns = cells.shape
    tiles = columns // LANES

    def step(index, carry):
        field = index // tiles
        at = pl.ds(pl.multiple_of((index % tiles) * LANES, LANES), LANES)
        extended = jnp.concatenate(
            [below[field, 0, :, at], cells[field, 0, :, at], above[field, 0, :, at]], axis=0
        )
        out[field, 0, :, at] = derivative(extended, 0)[HALO : HALO + rows]
        return carry

    lax.fori_loop(0, fields * tiles, step, 0)


def cut_kernel(count, pieces):
    def kernel(fields, *refs):
        outs, sems = refs[:-1], refs[-1]
        me = lax.axis_index("gy")
        copies = []
        for number, (hop, first, last) in enumerate(pieces):
            rows = outs[number].shape[2]
            at = pl.multiple_of(lax.rem(me + hop, count) * rows, rows)
            copy = pltpu.make_async_copy(fields.at[first:last, :, pl.ds(at, rows), :], outs[number], sems.at[number])
            copy.start()
            copies.append(copy)
        for copy in copies:
            copy.wait()

    return kernel


def terms(values):
    high = values.astype(jnp.bfloat16)
    rest = values - high.astype(jnp.float32)
    middle = rest.astype(jnp.bfloat16)
    low = (rest - middle.astype(jnp.float32)).astype(jnp.bfloat16)
    return (high, middle, low)


def product(one, other, pairs):
    total = None
    for i, j in pairs:
        term = jnp.dot(one[i], other[j], preferred_element_type=jnp.float32)
        total = term if total is None else total + term
    return total


FULL = ((2, 0), (0, 2), (1, 1), (1, 0), (0, 1), (0, 0))
SHORT = ((1, 0), (0, 1), (0, 0))


def y_kernel(count, places, starts, first_field, fields, spans, aliased):
    def kernel(*refs):
        number = len(places)
        blocks = dict(zip(places, refs))
        begin = dict(zip(places, starts))
        inner = [ref[...] for ref in refs[number : number + 3]]
        outer = [ref[...] for ref in refs[number + 3 : number + 6]]
        out, result, sems = refs[number + 6 + aliased :]
        _, _, rows, columns = refs[0].shape
        total = count * columns
        me = lax.axis_index("gy")
        copies = []

        def piece(lane):
            block, at = divmod(lane % total, columns)
            low = first_field - begin[block]
            return terms(blocks[block][low : low + fields, 0, :, at : at + LANES].reshape(fields * rows, LANES))

        def send(first, last, base):
            block, at = divmod(first % total, columns)
            to = pl.multiple_of(lax.rem(me + block, count) * columns + at, LANES)
            copy = pltpu.make_async_copy(
                result.at[:, :, :, pl.ds(base, last - first)],
                out.at[pl.ds(first_field, fields), :, :, pl.ds(to, last - first)],
                sems.at[len(copies)],
            )
            copy.start()
            copies.append(copy)

        size = fields * rows
        units, base = [], 0
        for first, last in spans:
            tile = {lane: piece(lane) for lane in range(first - LANES, last + LANES, LANES)}
            units += [(lane, base + lane - first, first, last, tile) for lane in range(first, last, UNIT)]
            base += last - first

        def stacked(shifts, term, group):
            return jnp.concatenate(
                [jnp.concatenate([tile[lane + s][term] for s in shifts], axis=1) for lane, _, _, _, tile in group], axis=0
            )

        together = max(1, STACK // size)
        sent = {first: first for first, _ in spans}
        for start in range(0, len(units), together):
            group = units[start : start + together]
            middle = [stacked((0, LANES), t, group) for t in range(3)]
            sides = [stacked((-LANES, UNIT), t, group) for t in range(2)]
            solved = product(sides, outer, SHORT) + product(middle, inner, FULL)
            for number, (lane, at, first, last, _) in enumerate(group):
                part = solved[number * size : (number + 1) * size]
                result[:, 0, :, at : at + UNIT] = part.reshape(fields, rows, UNIT)
                while sent[first] < last:
                    edge = min((sent[first] // columns + 1) * columns, last)
                    if edge > lane + UNIT:
                        break
                    send(sent[first], edge, at - lane + sent[first])
                    sent[first] = edge
        for copy in copies:
            copy.wait()

    return kernel


def y_call(parts, count, places, starts, first_field, fields, depth, spans, matrices, partial):
    operands = [*(parts[place] for place in places), *matrices]
    _, slab, rows, columns = operands[0].shape
    width = sum(last - first for first, last in spans)
    pieces = sum(-(-last // columns) - first // columns for first, last in spans)
    vmem = pl.BlockSpec(memory_space=pltpu.VMEM)
    hbm = pl.BlockSpec(memory_space=pl.ANY)
    aliased = partial is not None
    size = fields * rows * width
    return pl.pallas_call(
        y_kernel(count, places, starts, first_field, fields, spans, int(aliased)),
        out_shape=jax.ShapeDtypeStruct((depth, slab, rows, count * columns), jnp.float32),
        in_specs=[vmem] * len(operands) + [hbm] * aliased,
        out_specs=hbm,
        scratch_shapes=[
            pltpu.VMEM((fields, slab, rows, width), jnp.float32),
            pltpu.SemaphoreType.DMA((pieces,)),
        ],
        input_output_aliases={len(operands): 0} if aliased else {},
        compiler_params=pltpu.CompilerParams(vmem_limit_bytes=LIMIT),
        cost_estimate=pl.CostEstimate(
            flops=9 * 2 * 256 * size, bytes_accessed=8 * size, transcendentals=0
        ),
    )(*[pltpu.with_memory_space_constraint(x, pltpu.VMEM) for x in operands], *([partial] if aliased else []))


def split_band():
    matrix = band()
    inner = matrix[LANES : LANES + UNIT]
    outer = np.concatenate([matrix[:LANES], matrix[LANES + UNIT :]], axis=0)
    pieces = []
    for values in (inner, outer):
        for _ in range(3):
            piece = values.astype(jnp.bfloat16)
            values = values - piece.astype(np.float32)
            pieces.append(jnp.asarray(piece))
    return pieces


def body(fields):
    count = lax.axis_size("gy")
    ring = lax.axis_size("gx")
    depth, slab, rows, columns = fields.shape
    part = rows // count
    value = {}
    matrices = split_band()
    source = pltpu.with_memory_space_constraint(fields, pltpu.HBM)
    cuts = {}
    def piece_of(hop):
        name = "y%s" % hop
        if name[-1] == "p":
            return (int(hop[:-1]), 0, SPLIT)
        if name[-1] == "q":
            return (int(hop[:-1]), SPLIT, depth)
        return (int(hop), 0, depth)

    for group in GROUPS:
        pieces = [piece_of(str(hop)) for hop in group]
        got = pl.pallas_call(
            cut_kernel(count, pieces),
            out_shape=[
                jax.ShapeDtypeStruct((last - first, slab, part, columns), jnp.float32) for _, first, last in pieces
            ],
            in_specs=[pl.BlockSpec(memory_space=pl.ANY)],
            out_specs=[pl.BlockSpec(memory_space=pl.ANY)] * len(pieces),
            scratch_shapes=[pltpu.SemaphoreType.DMA((len(pieces),))],
            compiler_params=pltpu.CompilerParams(vmem_limit_bytes=2**20),
            cost_estimate=pl.CostEstimate(flops=0, bytes_accessed=2 * 4 * len(pieces) * depth * part * columns, transcendentals=0),
        )(source)
        cuts.update(zip((str(hop) for hop in group), got))
        if group is not GROUPS[-1]:
            fields, cuts[str(group[-1])] = lax.optimization_barrier((fields, cuts[str(group[-1])]))
            source = pltpu.with_memory_space_constraint(fields, pltpu.HBM)
    value["y0"] = cuts["0"]
    vmem = pl.BlockSpec(memory_space=pltpu.VMEM)
    c, e = columns, LANES
    inner = ((3 * c + e, 6 * c - e), (8 * c + e, 9 * c - e))
    ring_2 = ((2 * c + e, 3 * c + e), (6 * c - e, 7 * c - e))
    ring_1 = ((7 * c - e, 8 * c + e), (9 * c - e, 10 * c + e))
    plans = {
        "A": ([3, 4, 5, 0], inner, ""),
        "B": ([2, 3, 5, 6], ring_2, ""),
        "C": ([6, 7, 0, 1, 2], ring_1, "p" if SPLIT else ""),
        "D": ([6, 7, 0, 1, 2], ring_1, "q"),
    }
    last = None

    def tie(x, deps):
        for dep in deps:
            x, value[dep] = lax.optimization_barrier((x, value[dep]))
        return x

    for name, deps in STEPS:
        if name[0] == "y":
            hop = piece_of(name[1:])[0]
            cut = tie(cuts[name[1:]], deps)
            value[name] = lax.ppermute(cut, "gy", [(i, (i + hop) % count) for i in range(count)])
        elif name == "b":
            halo = tie(fields[:, :, rows - HALO :], deps)
            value[name] = lax.ppermute(halo, "gx", [(i, (i + 1) % ring) for i in range(ring)])
        elif name == "a":
            halo = tie(fields[:, :, :HALO], deps)
            value[name] = lax.ppermute(halo, "gx", [((i + 1) % ring, i) for i in range(ring)])
        elif name == "X":
            value[name] = pl.pallas_call(
                x_kernel,
                out_shape=jax.ShapeDtypeStruct(fields.shape, fields.dtype),
                in_specs=[vmem] * 3,
                out_specs=vmem,
                compiler_params=pltpu.CompilerParams(vmem_limit_bytes=XLIMIT),
                cost_estimate=pl.CostEstimate(
                    flops=20 * fields.size, bytes_accessed=8 * fields.size, transcendentals=0
                ),
            )(fields, tie(value["b"], deps), value["a"])
        else:
            places, spans, suffix = plans[name]
            low, high = {"": (0, depth), "p": (0, SPLIT), "q": (SPLIT, depth)}[suffix]
            parts, starts = {}, []
            for place in places:
                source_name = "y%d" % ((count - place) % count)
                if source_name in value:
                    starts.append(0)
                else:
                    source_name += suffix
                    starts.append(low)
                parts[place] = value[source_name]
            parts[places[0]] = tie(parts[places[0]], deps)
            last = y_call(parts, count, places, starts, low, high - low, depth, spans, matrices, last)
            value[name] = last
    return (value["X"], last)


def solution(mesh):
    placed = (P(None, "gz", "gx", "gy"),)
    return jax.shard_map(
        body,
        mesh=mesh,
        in_specs=placed,
        out_specs=(P(None, "gz", "gx", "gy"), P(None, "gz", ("gx", "gy"), None)),
        check_vma=False,
    )
```

```python
import jax
import jax.numpy as jnp
import numpy as np
from jax import lax
from jax.experimental import pallas as pl
from jax.experimental.pallas import tpu as pltpu
from jax.sharding import PartitionSpec as P

LEVELS = 4
HALO = 24
LIMIT = 8 * 2**20
STACK = 640
STEPS = (
    ("y4", ()),
    ("y3", ()),
    ("y5", ()),
    ("b", ()),
    ("a", ()),
    ("X", ()),
    ("y6", ("y4", "b", )),
    ("y2", ("y4", "a", )),
    ("y7p", ("y3", "X", )),
    ("y1p", ("y5", )),
    ("y7q", ("y3", )),
    ("y1q", ("y5", )),
    ("A", ()),
    ("B", ()),
    ("C", ()),
    ("D", ()),
)
GROUPS = ((4,), (3, 5), (2, 6, "1p", "7p", "1q", "7q", 0))
SPLIT = 3
XLIMIT = 12 * 2**20
LANES = 128
UNIT = 256
REACH = 17


def coefficients(levels):
    upper = 1.0 / 3.0
    middle = 1.0
    factors = []
    for level in range(levels):
        factor = upper / middle
        factors.append(factor)
        middle = middle - 2.0 * factor * upper
        upper = -factor * upper
    return (factors, middle)


def band():
    taps = np.zeros(2 * REACH + 1)
    for offset, weight in ((1, 7.0 / 9.0), (2, 1.0 / 36.0)):
        taps[REACH + offset] = weight
        taps[REACH - offset] = -weight
    factors, middle = coefficients(LEVELS)
    for level in range(LEVELS):
        stride = 2**level
        last = taps
        taps = last.copy()
        taps[stride:] -= factors[level] * last[:-stride]
        taps[:-stride] -= factors[level] * last[stride:]
    matrix = np.zeros((UNIT + 2 * LANES, UNIT))
    for column in range(UNIT):
        first = LANES + column - REACH
        matrix[first : first + 2 * REACH + 1, column] = taps / middle
    return matrix.astype(np.float32)


def derivative(cells, axis):
    length = cells.shape[axis]

    def shifted(values, offset):
        return pltpu.roll(values, (-offset) % length, axis)

    factors, middle = coefficients(LEVELS)
    values = 7.0 / 9.0 * (shifted(cells, 1) - shifted(cells, -1)) + 1.0 / 36.0 * (
        shifted(cells, 2) - shifted(cells, -2)
    )
    for level in range(LEVELS):
        stride = 2**level
        values = values - factors[level] * (shifted(values, stride) + shifted(values, -stride))
    return values * (1.0 / middle)


def x_kernel(cells, below, above, out):
    fields, _, rows, columns = cells.shape
    tiles = columns // LANES

    def step(index, carry):
        field = index // tiles
        at = pl.ds(pl.multiple_of((index % tiles) * LANES, LANES), LANES)
        extended = jnp.concatenate(
            [below[field, 0, :, at], cells[field, 0, :, at], above[field, 0, :, at]], axis=0
        )
        out[field, 0, :, at] = derivative(extended, 0)[HALO : HALO + rows]
        return carry

    lax.fori_loop(0, fields * tiles, step, 0)


def cut_kernel(count, pieces):
    def kernel(fields, *refs):
        outs, sems = refs[:-1], refs[-1]
        me = lax.axis_index("gy")
        copies = []
        for number, (hop, first, last) in enumerate(pieces):
            rows = outs[number].shape[2]
            at = pl.multiple_of(lax.rem(me + hop, count) * rows, rows)
            copy = pltpu.make_async_copy(fields.at[first:last, :, pl.ds(at, rows), :], outs[number], sems.at[number])
            copy.start()
            copies.append(copy)
        for copy in copies:
            copy.wait()

    return kernel


def terms(values):
    high = values.astype(jnp.bfloat16)
    rest = values - high.astype(jnp.float32)
    middle = rest.astype(jnp.bfloat16)
    low = (rest - middle.astype(jnp.float32)).astype(jnp.bfloat16)
    return (high, middle, low)


def product(one, other, pairs):
    total = None
    for i, j in pairs:
        term = jnp.dot(one[i], other[j], preferred_element_type=jnp.float32)
        total = term if total is None else total + term
    return total


FULL = ((2, 0), (0, 2), (1, 1), (1, 0), (0, 1), (0, 0))


def y_kernel(count, places, starts, first_field, fields, spans, aliased):
    def kernel(*refs):
        number = len(places)
        blocks = dict(zip(places, refs))
        begin = dict(zip(places, starts))
        inner = [ref[...] for ref in refs[number : number + 3]]
        outer = [ref[...] for ref in refs[number + 3 : number + 6]]
        out, result, sems = refs[number + 6 + aliased :]
        _, _, rows, columns = refs[0].shape
        total = count * columns
        me = lax.axis_index("gy")
        copies = []

        def piece(lane):
            block, at = divmod(lane % total, columns)
            low = first_field - begin[block]
            return terms(blocks[block][low : low + fields, 0, :, at : at + LANES].reshape(fields * rows, LANES))

        def send(first, last, base):
            block, at = divmod(first % total, columns)
            to = pl.multiple_of(lax.rem(me + block, count) * columns + at, LANES)
            copy = pltpu.make_async_copy(
                result.at[:, :, :, pl.ds(base, last - first)],
                out.at[pl.ds(first_field, fields), :, :, pl.ds(to, last - first)],
                sems.at[len(copies)],
            )
            copy.start()
            copies.append(copy)

        size = fields * rows
        units, base = [], 0
        for first, last in spans:
            tile = {lane: piece(lane) for lane in range(first - LANES, last + LANES, LANES)}
            units += [(lane, base + lane - first, first, last, tile) for lane in range(first, last, UNIT)]
            base += last - first

        def stacked(shifts, term, group):
            return jnp.concatenate(
                [jnp.concatenate([tile[lane + s][term] for s in shifts], axis=1) for lane, _, _, _, tile in group], axis=0
            )

        together = max(1, STACK // size)
        sent = {first: first for first, _ in spans}
        for start in range(0, len(units), together):
            group = units[start : start + together]
            middle = [stacked((0, LANES), t, group) for t in range(3)]
            sides = [stacked((-LANES, UNIT), t, group) for t in range(3)]
            solved = product(sides, outer, FULL) + product(middle, inner, FULL)
            for number, (lane, at, first, last, _) in enumerate(group):
                part = solved[number * size : (number + 1) * size]
                result[:, 0, :, at : at + UNIT] = part.reshape(fields, rows, UNIT)
                while sent[first] < last:
                    edge = min((sent[first] // columns + 1) * columns, last)
                    if edge > lane + UNIT:
                        break
                    send(sent[first], edge, at - lane + sent[first])
                    sent[first] = edge
        for copy in copies:
            copy.wait()

    return kernel


def y_call(parts, count, places, starts, first_field, fields, depth, spans, matrices, partial):
    operands = [*(parts[place] for place in places), *matrices]
    _, slab, rows, columns = operands[0].shape
    width = sum(last - first for first, last in spans)
    pieces = sum(-(-last // columns) - first // columns for first, last in spans)
    vmem = pl.BlockSpec(memory_space=pltpu.VMEM)
    hbm = pl.BlockSpec(memory_space=pl.ANY)
    aliased = partial is not None
    size = fields * rows * width
    return pl.pallas_call(
        y_kernel(count, places, starts, first_field, fields, spans, int(aliased)),
        out_shape=jax.ShapeDtypeStruct((depth, slab, rows, count * columns), jnp.float32),
        in_specs=[vmem] * len(operands) + [hbm] * aliased,
        out_specs=hbm,
        scratch_shapes=[
            pltpu.VMEM((fields, slab, rows, width), jnp.float32),
            pltpu.SemaphoreType.DMA((pieces,)),
        ],
        input_output_aliases={len(operands): 0} if aliased else {},
        compiler_params=pltpu.CompilerParams(vmem_limit_bytes=LIMIT),
        cost_estimate=pl.CostEstimate(
            flops=12 * 2 * 256 * size, bytes_accessed=8 * size, transcendentals=0
        ),
    )(*[pltpu.with_memory_space_constraint(x, pltpu.VMEM) for x in operands], *([partial] if aliased else []))


def split_band():
    matrix = band()
    inner = matrix[LANES : LANES + UNIT]
    outer = np.concatenate([matrix[:LANES], matrix[LANES + UNIT :]], axis=0)
    pieces = []
    for values in (inner, outer):
        for _ in range(3):
            piece = values.astype(jnp.bfloat16)
            values = values - piece.astype(np.float32)
            pieces.append(jnp.asarray(piece))
    return pieces


def body(fields):
    count = lax.axis_size("gy")
    ring = lax.axis_size("gx")
    depth, slab, rows, columns = fields.shape
    part = rows // count
    value = {}
    matrices = split_band()
    source = pltpu.with_memory_space_constraint(fields, pltpu.HBM)
    cuts = {}
    def piece_of(hop):
        name = "y%s" % hop
        if name[-1] == "p":
            return (int(hop[:-1]), 0, SPLIT)
        if name[-1] == "q":
            return (int(hop[:-1]), SPLIT, depth)
        return (int(hop), 0, depth)

    for group in GROUPS:
        pieces = [piece_of(str(hop)) for hop in group]
        got = pl.pallas_call(
            cut_kernel(count, pieces),
            out_shape=[
                jax.ShapeDtypeStruct((last - first, slab, part, columns), jnp.float32) for _, first, last in pieces
            ],
            in_specs=[pl.BlockSpec(memory_space=pl.ANY)],
            out_specs=[pl.BlockSpec(memory_space=pl.ANY)] * len(pieces),
            scratch_shapes=[pltpu.SemaphoreType.DMA((len(pieces),))],
            compiler_params=pltpu.CompilerParams(vmem_limit_bytes=2**20),
            cost_estimate=pl.CostEstimate(flops=0, bytes_accessed=2 * 4 * len(pieces) * depth * part * columns, transcendentals=0),
        )(source)
        cuts.update(zip((str(hop) for hop in group), got))
        if group is not GROUPS[-1]:
            fields, cuts[str(group[-1])] = lax.optimization_barrier((fields, cuts[str(group[-1])]))
            source = pltpu.with_memory_space_constraint(fields, pltpu.HBM)
    value["y0"] = cuts["0"]
    vmem = pl.BlockSpec(memory_space=pltpu.VMEM)
    c, e = columns, LANES
    inner = ((3 * c + e, 6 * c - e), (8 * c + e, 9 * c - e))
    ring_2 = ((2 * c + e, 3 * c + e), (6 * c - e, 7 * c - e))
    ring_1 = ((7 * c - e, 8 * c + e), (9 * c - e, 10 * c + e))
    plans = {
        "E": ([2, 3, 4, 5, 6, 0], ((2 * c + e, 7 * c - e), (8 * c + e, 9 * c - e)), ""),
        "A": ([3, 4, 5, 0], inner, ""),
        "B": ([2, 3, 5, 6], ring_2, ""),
        "C": ([6, 7, 0, 1, 2], ring_1, "p" if SPLIT else ""),
        "D": ([6, 7, 0, 1, 2], ring_1, "q"),
    }
    last = None

    def tie(x, deps):
        for dep in deps:
            x, value[dep] = lax.optimization_barrier((x, value[dep]))
        return x

    for name, deps in STEPS:
        if name[0] == "y":
            hop = piece_of(name[1:])[0]
            cut = tie(cuts[name[1:]], deps)
            value[name] = lax.ppermute(cut, "gy", [(i, (i + hop) % count) for i in range(count)])
        elif name == "b":
            halo = tie(fields[:, :, rows - HALO :], deps)
            value[name] = lax.ppermute(halo, "gx", [(i, (i + 1) % ring) for i in range(ring)])
        elif name == "a":
            halo = tie(fields[:, :, :HALO], deps)
            value[name] = lax.ppermute(halo, "gx", [((i + 1) % ring, i) for i in range(ring)])
        elif name == "X":
            value[name] = pl.pallas_call(
                x_kernel,
                out_shape=jax.ShapeDtypeStruct(fields.shape, fields.dtype),
                in_specs=[vmem] * 3,
                out_specs=vmem,
                compiler_params=pltpu.CompilerParams(vmem_limit_bytes=XLIMIT),
                cost_estimate=pl.CostEstimate(
                    flops=20 * fields.size, bytes_accessed=8 * fields.size, transcendentals=0
                ),
            )(fields, tie(value["b"], deps), value["a"])
        else:
            places, spans, suffix = plans[name]
            low, high = {"": (0, depth), "p": (0, SPLIT), "q": (SPLIT, depth)}[suffix]
            parts, starts = {}, []
            for place in places:
                source_name = "y%d" % ((count - place) % count)
                if source_name in value:
                    starts.append(0)
                else:
                    source_name += suffix
                    starts.append(low)
                parts[place] = value[source_name]
            parts[places[0]] = tie(parts[places[0]], deps)
            last = y_call(parts, count, places, starts, low, high - low, depth, spans, matrices, last)
            value[name] = last
    return (value["X"], last)


def solution(mesh):
    placed = (P(None, "gz", "gx", "gy"),)
    return jax.shard_map(
        body,
        mesh=mesh,
        in_specs=placed,
        out_specs=(P(None, "gz", "gx", "gy"), P(None, "gz", ("gx", "gy"), None)),
        check_vma=False,
    )
```

```python
import jax
import jax.numpy as jnp
import numpy as np
from jax import lax
from jax.experimental import pallas as pl
from jax.experimental.pallas import tpu as pltpu
from jax.sharding import PartitionSpec as P

LEVELS = 4
HALO = 24
LIMIT = 8 * 2**20
STACK = 640
STEPS = (
    ("y4", ()),
    ("b", ()),
    ("a", ()),
    ("X", ()),
    ("y3", ()),
    ("y5", ()),
    ("y2", ("y4", "b", )),
    ("y6", ("y4", "a", )),
    ("y1p", ("y3", "X", )),
    ("y7p", ("y5", )),
    ("y1q", ("y3", )),
    ("y7q", ("y5", )),
    ("A", ()),
    ("B", ()),
    ("C", ()),
    ("D", ()),
)
GROUPS = ((4,), (3, 5), (2, 6, "1p", "7p", "1q", "7q", 0))
SPLIT = 3
XLIMIT = 12 * 2**20
LANES = 128
UNIT = 256
REACH = 17


def coefficients(levels):
    upper = 1.0 / 3.0
    middle = 1.0
    factors = []
    for level in range(levels):
        factor = upper / middle
        factors.append(factor)
        middle = middle - 2.0 * factor * upper
        upper = -factor * upper
    return (factors, middle)


def band():
    taps = np.zeros(2 * REACH + 1)
    for offset, weight in ((1, 7.0 / 9.0), (2, 1.0 / 36.0)):
        taps[REACH + offset] = weight
        taps[REACH - offset] = -weight
    factors, middle = coefficients(LEVELS)
    for level in range(LEVELS):
        stride = 2**level
        last = taps
        taps = last.copy()
        taps[stride:] -= factors[level] * last[:-stride]
        taps[:-stride] -= factors[level] * last[stride:]
    matrix = np.zeros((UNIT + 2 * LANES, UNIT))
    for column in range(UNIT):
        first = LANES + column - REACH
        matrix[first : first + 2 * REACH + 1, column] = taps / middle
    return matrix.astype(np.float32)


def derivative(cells, axis):
    length = cells.shape[axis]

    def shifted(values, offset):
        return pltpu.roll(values, (-offset) % length, axis)

    factors, middle = coefficients(LEVELS)
    values = 7.0 / 9.0 * (shifted(cells, 1) - shifted(cells, -1)) + 1.0 / 36.0 * (
        shifted(cells, 2) - shifted(cells, -2)
    )
    for level in range(LEVELS):
        stride = 2**level
        values = values - factors[level] * (shifted(values, stride) + shifted(values, -stride))
    return values * (1.0 / middle)


def x_kernel(cells, below, above, out):
    fields, _, rows, columns = cells.shape
    tiles = columns // LANES

    def step(index, carry):
        field = index // tiles
        at = pl.ds(pl.multiple_of((index % tiles) * LANES, LANES), LANES)
        extended = jnp.concatenate(
            [below[field, 0, :, at], cells[field, 0, :, at], above[field, 0, :, at]], axis=0
        )
        out[field, 0, :, at] = derivative(extended, 0)[HALO : HALO + rows]
        return carry

    lax.fori_loop(0, fields * tiles, step, 0)


def cut_kernel(count, pieces):
    def kernel(fields, *refs):
        outs, sems = refs[:-1], refs[-1]
        me = lax.axis_index("gy")
        copies = []
        for number, (hop, first, last) in enumerate(pieces):
            rows = outs[number].shape[2]
            at = pl.multiple_of(lax.rem(me + hop, count) * rows, rows)
            copy = pltpu.make_async_copy(fields.at[first:last, :, pl.ds(at, rows), :], outs[number], sems.at[number])
            copy.start()
            copies.append(copy)
        for copy in copies:
            copy.wait()

    return kernel


def terms(values):
    high = values.astype(jnp.bfloat16)
    rest = values - high.astype(jnp.float32)
    middle = rest.astype(jnp.bfloat16)
    low = (rest - middle.astype(jnp.float32)).astype(jnp.bfloat16)
    return (high, middle, low)


def product(one, other, pairs):
    total = None
    for i, j in pairs:
        term = jnp.dot(one[i], other[j], preferred_element_type=jnp.float32)
        total = term if total is None else total + term
    return total


FULL = ((2, 0), (0, 2), (1, 1), (1, 0), (0, 1), (0, 0))


def y_kernel(count, places, starts, first_field, fields, spans, aliased):
    def kernel(*refs):
        number = len(places)
        blocks = dict(zip(places, refs))
        begin = dict(zip(places, starts))
        inner = [ref[...] for ref in refs[number : number + 3]]
        outer = [ref[...] for ref in refs[number + 3 : number + 6]]
        out, result, sems = refs[number + 6 + aliased :]
        _, _, rows, columns = refs[0].shape
        total = count * columns
        me = lax.axis_index("gy")
        copies = []

        def piece(lane):
            block, at = divmod(lane % total, columns)
            low = first_field - begin[block]
            return terms(blocks[block][low : low + fields, 0, :, at : at + LANES].reshape(fields * rows, LANES))

        def send(first, last, base):
            block, at = divmod(first % total, columns)
            to = pl.multiple_of(lax.rem(me + block, count) * columns + at, LANES)
            copy = pltpu.make_async_copy(
                result.at[:, :, :, pl.ds(base, last - first)],
                out.at[pl.ds(first_field, fields), :, :, pl.ds(to, last - first)],
                sems.at[len(copies)],
            )
            copy.start()
            copies.append(copy)

        size = fields * rows
        units, base = [], 0
        for first, last in spans:
            tile = {lane: piece(lane) for lane in range(first - LANES, last + LANES, LANES)}
            units += [(lane, base + lane - first, first, last, tile) for lane in range(first, last, UNIT)]
            base += last - first

        def stacked(shifts, term, group):
            return jnp.concatenate(
                [jnp.concatenate([tile[lane + s][term] for s in shifts], axis=1) for lane, _, _, _, tile in group], axis=0
            )

        together = max(1, STACK // size)
        sent = {first: first for first, _ in spans}
        for start in range(0, len(units), together):
            group = units[start : start + together]
            middle = [stacked((0, LANES), t, group) for t in range(3)]
            sides = [stacked((-LANES, UNIT), t, group) for t in range(3)]
            solved = product(sides, outer, FULL) + product(middle, inner, FULL)
            for number, (lane, at, first, last, _) in enumerate(group):
                part = solved[number * size : (number + 1) * size]
                result[:, 0, :, at : at + UNIT] = part.reshape(fields, rows, UNIT)
                while sent[first] < last:
                    edge = min((sent[first] // columns + 1) * columns, last)
                    if edge > lane + UNIT:
                        break
                    send(sent[first], edge, at - lane + sent[first])
                    sent[first] = edge
        for copy in copies:
            copy.wait()

    return kernel


def y_call(parts, count, places, starts, first_field, fields, depth, spans, matrices, partial):
    operands = [*(parts[place] for place in places), *matrices]
    _, slab, rows, columns = operands[0].shape
    width = sum(last - first for first, last in spans)
    pieces = sum(-(-last // columns) - first // columns for first, last in spans)
    vmem = pl.BlockSpec(memory_space=pltpu.VMEM)
    hbm = pl.BlockSpec(memory_space=pl.ANY)
    aliased = partial is not None
    size = fields * rows * width
    return pl.pallas_call(
        y_kernel(count, places, starts, first_field, fields, spans, int(aliased)),
        out_shape=jax.ShapeDtypeStruct((depth, slab, rows, count * columns), jnp.float32),
        in_specs=[vmem] * len(operands) + [hbm] * aliased,
        out_specs=hbm,
        scratch_shapes=[
            pltpu.VMEM((fields, slab, rows, width), jnp.float32),
            pltpu.SemaphoreType.DMA((pieces,)),
        ],
        input_output_aliases={len(operands): 0} if aliased else {},
        compiler_params=pltpu.CompilerParams(vmem_limit_bytes=LIMIT),
        cost_estimate=pl.CostEstimate(
            flops=12 * 2 * 256 * size, bytes_accessed=8 * size, transcendentals=0
        ),
    )(*[pltpu.with_memory_space_constraint(x, pltpu.VMEM) for x in operands], *([partial] if aliased else []))


def split_band():
    matrix = band()
    inner = matrix[LANES : LANES + UNIT]
    outer = np.concatenate([matrix[:LANES], matrix[LANES + UNIT :]], axis=0)
    pieces = []
    for values in (inner, outer):
        for _ in range(3):
            piece = values.astype(jnp.bfloat16)
            values = values - piece.astype(np.float32)
            pieces.append(jnp.asarray(piece))
    return pieces


def body(fields):
    count = lax.axis_size("gy")
    ring = lax.axis_size("gx")
    depth, slab, rows, columns = fields.shape
    part = rows // count
    value = {}
    matrices = split_band()
    source = pltpu.with_memory_space_constraint(fields, pltpu.HBM)
    cuts = {}
    def piece_of(hop):
        name = "y%s" % hop
        if name[-1] == "p":
            return (int(hop[:-1]), 0, SPLIT)
        if name[-1] == "q":
            return (int(hop[:-1]), SPLIT, depth)
        return (int(hop), 0, depth)

    for group in GROUPS:
        pieces = [piece_of(str(hop)) for hop in group]
        got = pl.pallas_call(
            cut_kernel(count, pieces),
            out_shape=[
                jax.ShapeDtypeStruct((last - first, slab, part, columns), jnp.float32) for _, first, last in pieces
            ],
            in_specs=[pl.BlockSpec(memory_space=pl.ANY)],
            out_specs=[pl.BlockSpec(memory_space=pl.ANY)] * len(pieces),
            scratch_shapes=[pltpu.SemaphoreType.DMA((len(pieces),))],
            compiler_params=pltpu.CompilerParams(vmem_limit_bytes=2**20),
            cost_estimate=pl.CostEstimate(flops=0, bytes_accessed=2 * 4 * len(pieces) * depth * part * columns, transcendentals=0),
        )(source)
        cuts.update(zip((str(hop) for hop in group), got))
        if group is not GROUPS[-1]:
            fields, cuts[str(group[-1])] = lax.optimization_barrier((fields, cuts[str(group[-1])]))
            source = pltpu.with_memory_space_constraint(fields, pltpu.HBM)
    value["y0"] = cuts["0"]
    vmem = pl.BlockSpec(memory_space=pltpu.VMEM)
    c, e = columns, LANES
    inner = ((3 * c + e, 6 * c - e), (8 * c + e, 9 * c - e))
    ring_2 = ((2 * c + e, 3 * c + e), (6 * c - e, 7 * c - e))
    ring_1 = ((7 * c - e, 8 * c + e), (9 * c - e, 10 * c + e))
    plans = {
        "E": ([2, 3, 4, 5, 6, 0], ((2 * c + e, 7 * c - e), (8 * c + e, 9 * c - e)), ""),
        "A": ([3, 4, 5, 0], inner, ""),
        "B": ([2, 3, 5, 6], ring_2, ""),
        "C": ([6, 7, 0, 1, 2], ring_1, "p" if SPLIT else ""),
        "D": ([6, 7, 0, 1, 2], ring_1, "q"),
    }
    last = None

    def tie(x, deps):
        for dep in deps:
            x, value[dep] = lax.optimization_barrier((x, value[dep]))
        return x

    for name, deps in STEPS:
        if name[0] == "y":
            hop = piece_of(name[1:])[0]
            cut = tie(cuts[name[1:]], deps)
            value[name] = lax.ppermute(cut, "gy", [(i, (i + hop) % count) for i in range(count)])
        elif name == "b":
            halo = tie(fields[:, :, rows - HALO :], deps)
            value[name] = lax.ppermute(halo, "gx", [(i, (i + 1) % ring) for i in range(ring)])
        elif name == "a":
            halo = tie(fields[:, :, :HALO], deps)
            value[name] = lax.ppermute(halo, "gx", [((i + 1) % ring, i) for i in range(ring)])
        elif name == "X":
            value[name] = pl.pallas_call(
                x_kernel,
                out_shape=jax.ShapeDtypeStruct(fields.shape, fields.dtype),
                in_specs=[vmem] * 3,
                out_specs=vmem,
                compiler_params=pltpu.CompilerParams(vmem_limit_bytes=XLIMIT),
                cost_estimate=pl.CostEstimate(
                    flops=20 * fields.size, bytes_accessed=8 * fields.size, transcendentals=0
                ),
            )(fields, tie(value["b"], deps), value["a"])
        else:
            places, spans, suffix = plans[name]
            low, high = {"": (0, depth), "p": (0, SPLIT), "q": (SPLIT, depth)}[suffix]
            parts, starts = {}, []
            for place in places:
                source_name = "y%d" % ((count - place) % count)
                if source_name in value:
                    starts.append(0)
                else:
                    source_name += suffix
                    starts.append(low)
                parts[place] = value[source_name]
            parts[places[0]] = tie(parts[places[0]], deps)
            last = y_call(parts, count, places, starts, low, high - low, depth, spans, matrices, last)
            value[name] = last
    return (value["X"], last)


def solution(mesh):
    placed = (P(None, "gz", "gx", "gy"),)
    return jax.shard_map(
        body,
        mesh=mesh,
        in_specs=placed,
        out_specs=(P(None, "gz", "gx", "gy"), P(None, "gz", ("gx", "gy"), None)),
        check_vma=False,
    )
```
